32 devices in a mesh: groups: 2 (over y), replica: 4 (over z), tensor: 4 (over x, core).
Axes of the slice: x: 2, y: 2, z: 4, core: 2. Of those that a mesh axis runs over, the one named last changes fastest.
Arguments:
- features: bfloat16 [512, 8192], P(('groups', 'replica'), 'tensor'), parts along dimension 0, may hold values from -6 to 6
- base_query: bfloat16 [512, 8192], P(('groups', 'replica'), 'tensor'), parts along dimension 0, may hold values from -128 to 128
- base_key_value: bfloat16 [512, 2, 1024], P(('groups', 'replica'), None, 'tensor'), parts along dimension 0, may hold values from -6 to 6
- cached_key_rows: bfloat16 [512, 64, 1024], P(('groups', 'replica'), None, 'tensor'), parts along dimension 0, may hold values from -5 to 5
- cached_value_rows: bfloat16 [512, 64, 1024], P(('groups', 'replica'), None, 'tensor'), parts along dimension 0, may hold values from -6 to 6
- cache_length: int32 [512], P(('groups', 'replica')), parts along dimension 0, may hold values from 2 to 64, as said below
- row_adapter_index: int32 [512], P(('groups', 'replica')), parts along dimension 0, may hold values from 0 to 63, as said below
- adapter_storage_slot: int32 [128], P('groups'), parts along dimension 0, may hold values from 0 to 63, as said below
- adapter_down_maps: bfloat16 [64, 48, 8192], P('replica', None, 'tensor'), may hold values from -0.0625 to 0.0625
- query_up_maps: bfloat16 [64, 16, 8192], P('replica', None, 'tensor'), may hold values from -0.75 to 0.75
- key_value_up_maps: bfloat16 [64, 16, 2, 1024], P('replica', None, None, 'tensor'), may hold values from -0.75 to 0.75
- output_down_maps: bfloat16 [64, 16, 8192], P('replica', None, 'tensor'), may hold values from -0.0625 to 0.0625
- output_up_maps: bfloat16 [64, 16, 8192], P('replica', None, 'tensor'), may hold values from -1.5 to 1.5
Outputs:
- context: bfloat16 [512, 8192], P(('groups', 'replica'), 'tensor'), parts along dimension 0
- output_adjustment: bfloat16 [512, 8192], P(('groups', 'replica'), 'tensor'), parts along dimension 0
The draws below stay inside these ranges and needn't reach their ends.
There are 2 independent parts, one for each index of `groups`. The reference program is written for one: setup_inputs(seed, part) draws one part's arguments, and reference() takes and returns one part's arrays. A program takes and returns all parts, laid end to end along the dimension named above; an argument that names none is the same for every part. Nothing has to cross between parts.
Inputs may be any that keep to these rules, and one draw needn't show every extreme that they name: `row_adapter_index`: adapter a is stored on replica adapter_storage_slot[a] // 16. In each aligned block of 64 rows (the rows of one replica) at most 32 rows use adapters stored on any one replica, and the adapters of one replica receive exactly 32 rows from every block. Each storage position once: adapter a is at position adapter_storage_slot[a] % 16 of the store of replica adapter_storage_slot[a] // 16. `cache_length`: some row of every aligned block of 64 rows attends to all 64 positions.
All inputs are finite; a program needn't handle non-finite values.
Results may differ from the reference program's by a relative error of at most 0.012.
Values may be sent and summed in bfloat16 or wider, within the bound.
A program may use at most 64 MiB of HBM per device.

```python
import math
import jax
import jax.numpy as jnp
from jax import lax

MODEL_WIDTH = 8192
H = 64
KVH = 8
HEAD_DIM = 128
ADAPTER_RANK = 16
OWN = 16
ROWS_DEV = 64
CTX = 64
QUERY_COLUMNS = 8192
KEY_COLUMNS = 1024
ADAPTER_TOTAL = 64
ROWS = 256
CAP = 32


def shared_cache_normals(key):
    return jnp.clip(jax.random.normal(key, (ROWS, CTX, KEY_COLUMNS), jnp.float32), -4.0, 4.0)


def placement_tables(key):
    perm_key, hot_key, ticket_key, local_key, extra_key = jax.random.split(key, 5)
    slot_table = jax.random.permutation(perm_key, ADAPTER_TOTAL).astype(jnp.int32)
    replicas = ADAPTER_TOTAL // OWN
    blocks = ROWS // ROWS_DEV
    hottest = jax.random.randint(hot_key, (), 0, replicas)

    def one_block(block_key):
        shuffle_key, mixing_key = jax.random.split(block_key)
        tickets = jax.random.permutation(shuffle_key, replicas * CAP) // CAP
        priority = jnp.where(tickets == hottest, 0, 1)
        ordered = tickets[jnp.argsort(priority, stable=True)][:ROWS_DEV]
        return ordered[jax.random.permutation(mixing_key, ROWS_DEV)]
    owners = jax.vmap(one_block)(jax.random.split(ticket_key, blocks)).reshape(ROWS)
    local_slot = jnp.minimum(jax.random.randint(local_key, (ROWS,), 0, OWN), jax.random.randint(extra_key, (ROWS,), 0, OWN))
    adapter_at = jnp.argsort(slot_table, stable=True)
    row_adapters = adapter_at[owners * OWN + local_slot]
    return (slot_table, row_adapters.astype(jnp.int32))


def draw_adapter_storage_slot(key, part):
    slot_table, row_adapters = placement_tables(key)
    return slot_table


def draw_row_adapter_index(key, part):
    slot_table, row_adapters = placement_tables(key)
    return row_adapters


def draw_cached_key_rows(key, part):
    normals = shared_cache_normals(key)
    return normals.astype(jnp.bfloat16)


def draw_base_query(key, part):
    own_key = jax.random.fold_in(key, 12)
    drawn = jnp.clip(jax.random.normal(own_key, (ROWS, QUERY_COLUMNS), jnp.float32), -4.0, 4.0)
    return drawn.astype(jnp.bfloat16)


def draw_cache_length(key, part):
    key = jax.random.fold_in(key, 13)
    first_key, second_key = jax.random.split(key)
    lengths = jax.random.randint(first_key, (ROWS,), 2, CTX + 1)
    longest = jax.random.randint(second_key, (ROWS // ROWS_DEV,), 0, ROWS_DEV)
    longest_hit = (jnp.arange(ROWS_DEV)[None, :] == longest[:, None]).reshape(ROWS)
    return jnp.where(longest_hit, CTX, lengths).astype(jnp.int32)


def shard_levels(stream_key, shape, pieces, low, top_value):
    level, own = 1.0, jax.random.fold_in(stream_key, 6)
    for position, blocks in pieces:
        steps = jnp.exp(jax.random.uniform(jax.random.fold_in(own, position), (blocks,), jnp.float32, low / len(pieces), top_value / len(pieces)))
        level = level * jnp.repeat(steps, shape[position] // blocks).reshape([-1 if axis == position else 1 for axis in range(len(shape))])
    return level


def centred(key, shape, scale, limit, cuts=(), kind=jnp.bfloat16):
    loudness = shard_levels(key, shape, cuts, -0.22, 0.18) if cuts else 1.0
    result = jax.random.normal(key, shape, jnp.float32) * scale * loudness
    return jnp.minimum(jnp.maximum(result, -limit), limit).astype(kind)


def setup_inputs(seed: int = 0, part: int = 0) -> dict:
    key_of = jax.random.split(jax.random.key(seed), 14)
    part_splits = jax.random.split(jax.random.fold_in(key_of[13], part), 14)
    return {
        "features": centred(part_splits[0], (ROWS, MODEL_WIDTH), 1.0, 6.0, ((0, 4), (1, 4))),
        "base_query": draw_base_query(jax.random.fold_in(jax.random.fold_in(key_of[13], part), 71), part),
        "base_key_value": centred(part_splits[2], (ROWS, 2, KEY_COLUMNS), 1.0, 6.0, ((0, 4), (2, 4))),
        "cached_key_rows": draw_cached_key_rows(jax.random.fold_in(jax.random.fold_in(key_of[13], part), 71), part),
        "cached_value_rows": centred(part_splits[4], (ROWS, CTX, KEY_COLUMNS), 1.0, 6.0, ((0, 4), (2, 4))),
        "cache_length": draw_cache_length(jax.random.fold_in(jax.random.fold_in(key_of[13], part), 71), part),
        "row_adapter_index": draw_row_adapter_index(jax.random.fold_in(jax.random.fold_in(key_of[13], part), 71), part),
        "adapter_storage_slot": draw_adapter_storage_slot(jax.random.fold_in(jax.random.fold_in(key_of[13], part), 71), part),
        "adapter_down_maps": centred(key_of[8], (ADAPTER_TOTAL, 3 * ADAPTER_RANK, MODEL_WIDTH), MODEL_WIDTH ** -0.5, 0.0625, ((0, 4), (2, 4))),
        "query_up_maps": centred(key_of[9], (ADAPTER_TOTAL, ADAPTER_RANK, QUERY_COLUMNS), 0.125, 0.75, ((0, 4), (2, 4))),
        "key_value_up_maps": centred(key_of[10], (ADAPTER_TOTAL, ADAPTER_RANK, 2, KEY_COLUMNS), 0.125, 0.75, ((0, 4), (3, 4))),
        "output_down_maps": centred(key_of[11], (ADAPTER_TOTAL, ADAPTER_RANK, QUERY_COLUMNS), QUERY_COLUMNS ** -0.5, 0.0625, ((0, 4), (2, 4))),
        "output_up_maps": centred(key_of[12], (ADAPTER_TOTAL, ADAPTER_RANK, MODEL_WIDTH), 0.25, 1.5, ((0, 4), (2, 4))),
    }


adapter_scale = 2.0
masked_score = -1e+30

def attend(query_plain, query_correction, cache_key_rows, cache_values, current_key, fresh_value, length):
    highest_precision = lax.Precision.HIGHEST
    inverse_root = 1.0 / math.sqrt(HEAD_DIM)
    cache_score_rows = (jnp.einsum('box,qbx->boq', query_plain, cache_key_rows, precision=highest_precision) + adapter_scale * jnp.einsum('box,qbx->boq', query_correction, cache_key_rows, precision=highest_precision)) * inverse_root
    self_scores = (jnp.einsum('etp,ep->et', query_plain, current_key, precision=highest_precision) + adapter_scale * jnp.einsum('etp,ep->et', query_correction, current_key, precision=highest_precision)) * inverse_root
    is_valid = (jnp.arange(CTX) < length)[None, None, :]
    cache_score_rows = jnp.where(is_valid, cache_score_rows, masked_score)
    row_peak = jnp.maximum(lax.optimization_barrier(jnp.max(cache_score_rows, axis=2)), self_scores)
    cache_exp = jnp.where(is_valid, jnp.exp(cache_score_rows - row_peak[..., None]), 0.0)
    own_exp = jnp.exp(self_scores - row_peak)
    row_total = lax.optimization_barrier(jnp.sum(cache_exp, axis=2)) + own_exp
    cache_weights = (cache_exp / row_total[..., None]).astype(jnp.bfloat16)
    own_weights = (own_exp / row_total).astype(jnp.bfloat16)
    context = jnp.einsum('kgp,pkd->kgd', cache_weights.astype(jnp.float32), cache_values, precision=highest_precision)
    context = context + own_weights.astype(jnp.float32)[..., None] * fresh_value[:, None, :]
    return context.astype(jnp.bfloat16)

def reference(features, base_query, base_key_value, cached_key_rows, cached_value_rows, cache_length, row_adapter_index, adapter_storage_slot, adapter_down_maps, query_up_maps, key_value_up_maps, output_down_maps, output_up_maps):
    group_size = H // KVH
    row_slots = adapter_storage_slot[row_adapter_index]

    def one_row(packed):
        row_storage_slot, feature_row, query_row, key_value_row, keys_row, values_row, length = packed
        adapter_coefficients = jnp.dot(adapter_down_maps[row_storage_slot], feature_row, preferred_element_type=jnp.float32).astype(jnp.bfloat16)
        query_adjustment = jnp.dot(adapter_coefficients[:ADAPTER_RANK], query_up_maps[row_storage_slot], preferred_element_type=jnp.float32).astype(jnp.bfloat16)
        paired_maps = key_value_up_maps[row_storage_slot]
        key_adjustment = jnp.dot(adapter_coefficients[ADAPTER_RANK:2 * ADAPTER_RANK], paired_maps[:, 0, :], preferred_element_type=jnp.float32).astype(jnp.bfloat16)
        value_adjustment = jnp.dot(adapter_coefficients[2 * ADAPTER_RANK:], paired_maps[:, 1, :], preferred_element_type=jnp.float32).astype(jnp.bfloat16)
        newest_key = (key_value_row[0].astype(jnp.float32) + adapter_scale * key_adjustment.astype(jnp.float32)).astype(jnp.bfloat16)
        newest_value = (key_value_row[1].astype(jnp.float32) + adapter_scale * value_adjustment.astype(jnp.float32)).astype(jnp.bfloat16)
        context = attend(query_row.reshape(KVH, group_size, HEAD_DIM).astype(jnp.float32), query_adjustment.reshape(KVH, group_size, HEAD_DIM).astype(jnp.float32), keys_row.reshape(CTX, KVH, HEAD_DIM).astype(jnp.float32), values_row.reshape(CTX, KVH, HEAD_DIM).astype(jnp.float32), newest_key.reshape(KVH, HEAD_DIM).astype(jnp.float32), newest_value.reshape(KVH, HEAD_DIM).astype(jnp.float32), length).reshape(QUERY_COLUMNS)
        output_coefficients = jnp.dot(output_down_maps[row_storage_slot], context, preferred_element_type=jnp.float32).astype(jnp.bfloat16)
        output_adjustment = (adapter_scale * jnp.dot(output_coefficients, output_up_maps[row_storage_slot], preferred_element_type=jnp.float32)).astype(jnp.bfloat16)
        return (context, output_adjustment)
    context, output_adjustment = lax.map(one_row, (row_slots, features, base_query, base_key_value, cached_key_rows, cached_value_rows, cache_length))
    return (context, output_adjustment)
```

```python
import functools
import math

import jax
import jax.numpy as jnp
from jax import lax
from jax.experimental import pallas as pl
from jax.experimental.pallas import tpu as pltpu
from jax.sharding import PartitionSpec as P

HEAD_DIM = 128
LANES = 128
BLOCK_ROWS = 4

adapter_scale = 2.0
masked_score = -1e30
BF16 = jnp.bfloat16
F32 = jnp.float32

NN = (((1,), (0,)), ((), ()))
NT = (((1,), (1,)), ((), ()))


def mm(a, b, dims=NN):
    return lax.dot_general(a, b, dims, preferred_element_type=F32)


def iota(shape, dim):
    return lax.broadcasted_iota(jnp.int32, shape, dim)


def one_hot(hit):
    return jnp.where(hit, 1.0, 0.0).astype(BF16)


def kernel(
    replicas,
    tensors,
    cap,
    rank,
    index_ref,
    table_ref,
    length_ref,
    feature_ref,
    query_ref,
    key_value_ref,
    key_hbm,
    value_hbm,
    down_hbm,
    query_up_hbm,
    key_value_up_hbm,
    out_down_hbm,
    out_up_hbm,
    context_ref,
    adjust_ref,
    keys,
    values,
    down,
    query_up,
    key_value_up,
    out_down,
    out_up,
    feature_send,
    feature_recv,
    coeff_recv,
    delta_send,
    delta_recv,
    context_send,
    context_recv,
    out_coeff_recv,
    adjust_send,
    adjust_recv,
    base_heads,
    delta_heads,
    context_heads,
    base_scores,
    load_sems,
    feature_sems,
    coeff_sems,
    delta_sems,
    context_sems,
    out_coeff_sems,
    adjust_sems,
):
    n_rows, width = feature_ref.shape
    query_width = query_ref.shape[1]
    kv_width = key_value_ref.shape[1] // 2
    groups = kv_width // HEAD_DIM
    heads = query_width // HEAD_DIM // groups
    group_width = heads * HEAD_DIM
    positions = key_hbm.shape[1]
    adapters = table_ref.shape[1]
    own = out_down_hbm.shape[0] // rank
    slots = replicas * cap
    inverse_root = 1.0 / math.sqrt(HEAD_DIM)
    me = lax.axis_index("replica")
    my_tensor = lax.axis_index("tensor")

    def ahead(k):
        return lax.rem(me + k, replicas)

    def behind(k):
        return lax.rem(me + replicas - k, replicas)

    loads = []
    for i, (source, target) in enumerate(
        (
            (key_hbm, keys),
            (down_hbm, down),
            (value_hbm, values),
            (query_up_hbm, query_up),
            (key_value_up_hbm, key_value_up),
            (out_down_hbm, out_down),
            (out_up_hbm, out_up),
        )
    ):
        load = pltpu.make_async_copy(source, target, load_sems.at[i])
        load.start()
        loads.append(load)
    (
        keys_load,
        down_load,
        values_load,
        query_up_load,
        key_value_up_load,
        out_down_load,
        out_up_load,
    ) = loads

    barrier = pltpu.get_barrier_semaphore()
    for k in range(1, replicas):
        pl.semaphore_signal(
            barrier,
            inc=1,
            device_id={"replica": ahead(k)},
            device_id_type=pl.DeviceIdType.MESH,
        )
    for t in range(1, tensors):
        pl.semaphore_signal(
            barrier,
            inc=1,
            device_id={"tensor": lax.rem(my_tensor + t, tensors)},
            device_id_type=pl.DeviceIdType.MESH,
        )

    def remote(source, target, sems, i, device):
        copy = pltpu.make_async_remote_copy(
            src_ref=source,
            dst_ref=target,
            send_sem=sems.at[0, i],
            recv_sem=sems.at[1, i],
            device_id=device,
            device_id_type=pl.DeviceIdType.MESH,
        )
        copy.start()
        return copy

    table = table_ref[...]
    table_owner = table // own
    table_local = table - table_owner * own
    pair = jnp.where(iota((8, adapters), 0) == 0, table_owner, table_local)
    adapter_hits = one_hot(iota((adapters, n_rows), 0) == index_ref[...])
    looked_up = mm(pair.astype(F32).astype(BF16), adapter_hits).astype(jnp.int32)
    owner = looked_up[0:1]
    local_slot = looked_up[1:2]
    relative = owner - me
    relative = jnp.where(relative < 0, relative + replicas, relative)
    replica_rows = max(8, replicas)
    owner_hits = iota((replica_rows, n_rows), 0) == relative
    before = one_hot(iota((n_rows, n_rows), 0) <= iota((n_rows, n_rows), 1))
    counts = mm(one_hot(owner_hits), before)
    row_rank = jnp.sum(jnp.where(owner_hits, counts, 0.0), axis=0, keepdims=True) - 1.0
    row_target = relative * cap + row_rank.astype(jnp.int32)
    placing = one_hot(iota((slots, n_rows), 0) == row_target)
    identity = one_hot(iota((n_rows, n_rows), 0) == iota((n_rows, n_rows), 1))
    unplacing = mm(identity, placing, NT).astype(BF16)
    slot_hits = one_hot(iota((LANES, n_rows), 0) == local_slot)
    selectors = mm(placing, slot_hits, NT).astype(BF16)

    packed = mm(placing, feature_ref[...]).astype(BF16)
    feature_recv[0, :, :width] = packed[:cap]
    feature_recv[0, :, width:] = selectors[:cap]
    for k in range(1, replicas):
        feature_send[k, :, :width] = packed[k * cap : (k + 1) * cap]
        feature_send[k, :, width:] = selectors[k * cap : (k + 1) * cap]
    pl.semaphore_wait(barrier, replicas + tensors - 2)
    feature_copies = [None] + [
        remote(
            feature_send.at[k], feature_recv.at[k], feature_sems, k, {"replica": ahead(k)}
        )
        for k in range(1, replicas)
    ]

    score_rows = n_rows * heads
    block_columns = BLOCK_ROWS * positions
    block_heads = BLOCK_ROWS * heads
    for g in range(groups):
        for h in range(heads):
            column = (g * heads + h) * HEAD_DIM
            base_heads[g, pl.ds(h, n_rows, stride=heads), :] = query_ref[
                :, column : column + HEAD_DIM
            ].astype(F32)
    blocks = n_rows // BLOCK_ROWS
    step_blocks = min(8, blocks)
    steps = blocks // step_blocks
    step_rows = step_blocks * BLOCK_ROWS
    step_heads = step_blocks * block_heads

    def block_of(ref, step, g):
        block = ref[
            pl.ds(pl.multiple_of(step * step_rows, step_rows), step_rows),
            :,
            g * HEAD_DIM : (g + 1) * HEAD_DIM,
        ]
        return block.reshape(step_blocks, block_columns, HEAD_DIM)

    def heads_of(step):
        return pl.ds(pl.multiple_of(step * step_heads, step_heads), step_heads)

    def score(query, key):
        return lax.dot_general(
            query.reshape(step_blocks, block_heads, HEAD_DIM),
            key,
            (((2,), (2,)), ((0,), (0,))),
            preferred_element_type=F32,
        ).reshape(step_heads, block_columns)

    def row_hits(step):
        head_row = iota((step_heads, n_rows), 0) // heads + step * step_rows
        return head_row == iota((step_heads, n_rows), 1)

    lengths = length_ref[...].astype(F32)
    keys_load.wait()

    def base_step(step, carry):
        spread = jnp.where(row_hits(step), lengths, 0.0).astype(BF16)
        head_lengths = mm(spread, jnp.ones((n_rows, block_columns), BF16))
        column = iota((step_heads, block_columns), 1)
        row = iota((step_heads, block_columns), 0)
        valid = ((row // heads) % BLOCK_ROWS == column // positions) & (
            (column % positions).astype(F32) < head_lengths
        )
        for g in range(groups):
            found = score(base_heads[g, heads_of(step), :].astype(BF16), block_of(keys, step, g))
            base_scores[g, heads_of(step), :] = jnp.where(
                valid, found * inverse_root, masked_score
            )
        return carry

    lax.fori_loop(0, steps, base_step, 0)

    bundles = [[k] for k in range(replicas)] if replicas <= 4 else [list(range(replicas))]
    down_load.wait()
    coeff_parts = []
    selector_parts = []
    chooser = one_hot(iota((own, LANES), 0) == iota((own, LANES), 1))

    def fold(terms, selector):
        stacked = terms.reshape(own, terms.shape[0] // own, terms.shape[1])
        return jnp.sum(stacked * selector[:, None, :], axis=0)

    for bundle in bundles:
        for k in bundle:
            if k:
                feature_copies[k].wait()
        received = feature_recv[bundle[0] : bundle[-1] + 1].reshape(len(bundle) * cap, -1)
        selector = mm(chooser, received[:, width:], NT)
        selector_parts.append(selector)
        coeff_parts.append(fold(mm(down[...], received[:, :width], NT), selector))
    selector = jnp.concatenate(selector_parts, axis=1)

    def sum_over_tensor(parts, recv, sems):
        for bundle, part in zip(bundles, parts):
            recv[0, :, bundle[0] * cap : (bundle[-1] + 1) * cap] = part
        copies = [
            remote(
                recv.at[0],
                recv.at[t],
                sems,
                t,
                {"tensor": lax.rem(my_tensor + t, tensors)},
            )
            for t in range(1, tensors)
        ]
        for copy in copies:
            copy.wait()
        total = recv[0]
        for t in range(1, tensors):
            total = total + recv[t]
        return total.astype(BF16).astype(F32)

    def expand(coeffs):
        spread = selector[:, None, :] * coeffs[None, :, :]
        return spread.reshape(own * rank, slots).T.astype(BF16)

    coeffs = sum_over_tensor(coeff_parts, coeff_recv, coeff_sems)
    query_coeffs = expand(coeffs[:rank])
    key_coeffs = expand(coeffs[rank : 2 * rank])
    value_coeffs = expand(coeffs[2 * rank :])

    query_up_load.wait()
    key_value_up_load.wait()
    delta_copies = []
    for g in range(groups):
        sent = [
            mm(query_coeffs, query_up[:, g * group_width : (g + 1) * group_width]),
            mm(key_coeffs, key_value_up[:, g * HEAD_DIM : (g + 1) * HEAD_DIM]),
            mm(
                value_coeffs,
                key_value_up[:, kv_width + g * HEAD_DIM : kv_width + (g + 1) * HEAD_DIM],
            ),
        ]
        sent = jnp.concatenate([x.astype(BF16) for x in sent], axis=1)
        delta_recv[g, 0] = sent[:cap]
        for k in range(1, replicas):
            delta_send[g, k] = sent[k * cap : (k + 1) * cap]
        delta_copies.append(
            [None]
            + [
                remote(
                    delta_send.at[g, k],
                    delta_recv.at[g, k],
                    delta_sems.at[g],
                    k,
                    {"replica": behind(k)},
                )
                for k in range(1, replicas)
            ]
        )

    values_load.wait()
    context_copies = []
    for g in range(groups):
        for k in range(1, replicas):
            delta_copies[g][k].wait()
        deltas = mm(unplacing, delta_recv[g].reshape(slots, -1))
        for h in range(heads):
            delta_heads[pl.ds(h, n_rows, stride=heads), :] = deltas[
                :, h * HEAD_DIM : (h + 1) * HEAD_DIM
            ]
        column = g * HEAD_DIM
        new_key = (
            key_value_ref[:, column : column + HEAD_DIM].astype(F32)
            + adapter_scale * deltas[:, group_width : group_width + HEAD_DIM]
        ).astype(BF16)
        new_value = (
            key_value_ref[:, kv_width + column : kv_width + column + HEAD_DIM].astype(F32)
            + adapter_scale * deltas[:, group_width + HEAD_DIM :]
        ).astype(BF16)

        def attend_step(step, carry, g=g, new_key=new_key, new_value=new_value):
            here = heads_of(step)
            plain = base_heads[g, here, :].astype(BF16)
            correction = delta_heads[here, :].astype(BF16)
            scores = base_scores[g, here, :] + (adapter_scale * inverse_root) * score(
                correction, block_of(keys, step, g)
            )
            own_scores = (
                mm(plain, new_key, NT) + adapter_scale * mm(correction, new_key, NT)
            ) * inverse_root
            own_scores = jnp.where(row_hits(step), own_scores, masked_score)
            peak = jnp.maximum(
                jnp.max(scores, axis=1, keepdims=True), jnp.max(own_scores, axis=1, keepdims=True)
            )
            cache_exp = jnp.exp(scores - peak)
            own_exp = jnp.exp(own_scores - peak)
            total = jnp.sum(cache_exp, axis=1, keepdims=True) + jnp.sum(
                own_exp, axis=1, keepdims=True
            )
            share = 1.0 / total
            weights = (cache_exp * share).astype(BF16)
            own_weights = (own_exp * share).astype(BF16)
            found = lax.dot_general(
                weights.reshape(step_blocks, block_heads, block_columns),
                block_of(values, step, g),
                (((2,), (1,)), ((0,), (0,))),
                preferred_element_type=F32,
            ).reshape(step_heads, HEAD_DIM)
            context_heads[here, :] = found + mm(own_weights, new_value)
            return carry

        lax.fori_loop(0, steps, attend_step, 0)
        for h in range(heads):
            column = (g * heads + h) * HEAD_DIM
            context_ref[:, column : column + HEAD_DIM] = context_heads[
                pl.ds(h, n_rows, stride=heads), :
            ].astype(BF16)
        packed = mm(placing, context_ref[:, g * group_width : (g + 1) * group_width]).astype(BF16)
        context_recv[g, 0] = packed[:cap]
        for k in range(1, replicas):
            context_send[g, k] = packed[k * cap : (k + 1) * cap]
        context_copies.append(
            [None]
            + [
                remote(
                    context_send.at[g, k],
                    context_recv.at[g, k],
                    context_sems.at[g],
                    k,
                    {"replica": ahead(k)},
                )
                for k in range(1, replicas)
            ]
        )

    out_down_load.wait()
    out_terms = [0.0 for _ in bundles]
    for g in range(groups):
        for i, bundle in enumerate(bundles):
            for k in bundle:
                if k:
                    context_copies[g][k].wait()
            received = context_recv[g, bundle[0] : bundle[-1] + 1].reshape(len(bundle) * cap, -1)
            out_terms[i] = out_terms[i] + mm(
                out_down[:, g * group_width : (g + 1) * group_width], received, NT
            )
    out_parts = [fold(terms, part) for terms, part in zip(out_terms, selector_parts)]
    out_coeffs = expand(sum_over_tensor(out_parts, out_coeff_recv, out_coeff_sems))
    out_up_load.wait()
    adjust_copies = []
    for g in range(groups):
        sent = (
            adapter_scale * mm(out_coeffs, out_up[:, g * group_width : (g + 1) * group_width])
        ).astype(BF16)
        adjust_recv[g, 0] = sent[:cap]
        for k in range(1, replicas):
            adjust_send[g, k] = sent[k * cap : (k + 1) * cap]
        adjust_copies.append(
            [None]
            + [
                remote(
                    adjust_send.at[g, k],
                    adjust_recv.at[g, k],
                    adjust_sems.at[g],
                    k,
                    {"replica": behind(k)},
                )
                for k in range(1, replicas)
            ]
        )
    for g in range(groups):
        for k in range(1, replicas):
            adjust_copies[g][k].wait()
        adjust_ref[:, g * group_width : (g + 1) * group_width] = mm(
            unplacing, adjust_recv[g].reshape(slots, -1)
        ).astype(BF16)


def local(
    replicas,
    tensors,
    features,
    base_query,
    base_key_value,
    cached_key_rows,
    cached_value_rows,
    cache_length,
    row_adapter_index,
    adapter_storage_slot,
    adapter_down_maps,
    query_up_maps,
    key_value_up_maps,
    output_down_maps,
    output_up_maps,
):
    n_rows, width = features.shape
    own, coeff_width, _ = adapter_down_maps.shape
    rank = coeff_width // 3
    query_width = base_query.shape[1]
    kv_width = base_key_value.shape[2]
    positions = cached_key_rows.shape[1]
    groups = kv_width // HEAD_DIM
    heads = query_width // HEAD_DIM // groups
    group_width = heads * HEAD_DIM
    capacity = min(n_rows // 2, 2 * n_rows // replicas)
    cap = -(-capacity // 16) * 16
    slots = replicas * cap
    score_rows = n_rows * heads

    vmem = pl.BlockSpec(memory_space=pltpu.VMEM)
    anywhere = pl.BlockSpec(memory_space=pl.ANY)

    def pair_sems(*lead):
        return pltpu.SemaphoreType.DMA((*lead, 2, replicas))

    return pl.pallas_call(
        functools.partial(kernel, replicas, tensors, cap, rank),
        out_shape=(
            jax.ShapeDtypeStruct((n_rows, query_width), BF16),
            jax.ShapeDtypeStruct((n_rows, query_width), BF16),
        ),
        in_specs=[vmem] * 6 + [anywhere] * 7,
        out_specs=(vmem, vmem),
        scratch_shapes=[
            pltpu.VMEM(cached_key_rows.shape, BF16),
            pltpu.VMEM(cached_value_rows.shape, BF16),
            pltpu.VMEM((own * coeff_width, width), BF16),
            pltpu.VMEM((own * rank, query_width), BF16),
            pltpu.VMEM((own * rank, 2 * kv_width), BF16),
            pltpu.VMEM((own * rank, query_width), BF16),
            pltpu.VMEM((own * rank, query_width), BF16),
            pltpu.VMEM((replicas, cap, width + LANES), BF16),
            pltpu.VMEM((replicas, cap, width + LANES), BF16),
            pltpu.VMEM((tensors, coeff_width, slots), F32),
            pltpu.VMEM((groups, replicas, cap, group_width + 2 * HEAD_DIM), BF16),
            pltpu.VMEM((groups, replicas, cap, group_width + 2 * HEAD_DIM), BF16),
            pltpu.VMEM((groups, replicas, cap, group_width), BF16),
            pltpu.VMEM((groups, replicas, cap, group_width), BF16),
            pltpu.VMEM((tensors, rank, slots), F32),
            pltpu.VMEM((groups, replicas, cap, group_width), BF16),
            pltpu.VMEM((groups, replicas, cap, group_width), BF16),
            pltpu.VMEM((groups, score_rows, HEAD_DIM), F32),
            pltpu.VMEM((score_rows, HEAD_DIM), F32),
            pltpu.VMEM((score_rows, HEAD_DIM), F32),
            pltpu.VMEM((groups, score_rows, BLOCK_ROWS * positions), F32),
            pltpu.SemaphoreType.DMA((7,)),
            pair_sems(),
            pltpu.SemaphoreType.DMA((2, tensors)),
            pair_sems(groups),
            pair_sems(groups),
            pltpu.SemaphoreType.DMA((2, tensors)),
            pair_sems(groups),
        ],
        compiler_params=pltpu.CompilerParams(
            collective_id=0, has_side_effects=True, vmem_limit_bytes=56 * 1024 * 1024
        ),
    )(
        row_adapter_index.reshape(1, -1),
        adapter_storage_slot.reshape(1, -1),
        cache_length.reshape(1, -1),
        features,
        base_query,
        base_key_value.reshape(n_rows, 2 * kv_width),
        cached_key_rows,
        cached_value_rows,
        adapter_down_maps.reshape(own * coeff_width, width),
        query_up_maps.reshape(own * rank, query_width),
        key_value_up_maps.reshape(own * rank, 2 * kv_width),
        output_down_maps.reshape(own * rank, query_width),
        output_up_maps.reshape(own * rank, query_width),
    )


def solution(mesh):
    return jax.shard_map(
        functools.partial(local, mesh.shape["replica"], mesh.shape["tensor"]),
        mesh=mesh,
        in_specs=(
            P(("groups", "replica"), "tensor"),
            P(("groups", "replica"), "tensor"),
            P(("groups", "replica"), None, "tensor"),
            P(("groups", "replica"), None, "tensor"),
            P(("groups", "replica"), None, "tensor"),
            P(("groups", "replica")),
            P(("groups", "replica")),
            P("groups"),
            P("replica", None, "tensor"),
            P("replica", None, "tensor"),
            P("replica", None, None, "tensor"),
            P("replica", None, "tensor"),
            P("replica", None, "tensor"),
        ),
        out_specs=(P(("groups", "replica"), "tensor"), P(("groups", "replica"), "tensor")),
        check_vma=False,
    )
```

```python
import functools
import math

import jax
import jax.numpy as jnp
from jax import lax
from jax.experimental import pallas as pl
from jax.experimental.pallas import tpu as pltpu
from jax.sharding import PartitionSpec as P

HEAD_DIM = 128
LANES = 128
BLOCK_ROWS = 4

adapter_scale = 2.0
masked_score = -1e30
BF16 = jnp.bfloat16
F32 = jnp.float32

NN = (((1,), (0,)), ((), ()))
NT = (((1,), (1,)), ((), ()))


def mm(a, b, dims=NN):
    return lax.dot_general(a, b, dims, preferred_element_type=F32)


def iota(shape, dim):
    return lax.broadcasted_iota(jnp.int32, shape, dim)


def one_hot(hit):
    return jnp.where(hit, 1.0, 0.0).astype(BF16)


def kernel(
    replicas,
    tensors,
    cap,
    halves,
    rank,
    index_ref,
    table_ref,
    length_ref,
    feature_ref,
    query_ref,
    key_value_ref,
    key_hbm,
    value_hbm,
    down_hbm,
    query_up_hbm,
    key_value_up_hbm,
    out_down_hbm,
    out_up_hbm,
    context_ref,
    adjust_recv,
    unplacing_ref,
    keys,
    values,
    down,
    query_up,
    key_value_up,
    key_value_split,
    out_down,
    out_up,
    feature_send,
    feature_recv,
    coeff_recv,
    delta_send,
    delta_recv,
    context_send,
    context_recv,
    out_coeff_recv,
    adjust_send,
    base_heads,
    delta_heads,
    context_heads,
    base_scores,
    load_sems,
    feature_sems,
    coeff_sems,
    delta_sems,
    context_sems,
    out_coeff_sems,
    adjust_sems,
    keep_sems,
):
    n_rows, width = feature_ref.shape
    query_width = query_ref.shape[1]
    kv_width = key_value_ref.shape[2]
    groups = kv_width // HEAD_DIM
    heads = query_width // HEAD_DIM // groups
    group_width = heads * HEAD_DIM
    positions = key_hbm.shape[1]
    adapters = table_ref.shape[1]
    own = out_down_hbm.shape[0] // rank
    half_cap = cap // halves
    half_slots = replicas * half_cap
    slots = replicas * cap
    inverse_root = 1.0 / math.sqrt(HEAD_DIM)
    me = lax.axis_index("replica")
    my_tensor = lax.axis_index("tensor")

    def ahead(k):
        return lax.rem(me + k, replicas)

    def behind(k):
        return lax.rem(me + replicas - k, replicas)

    loads = []
    for i, (source, target) in enumerate(
        (
            (key_hbm, keys),
            (down_hbm, down),
            (value_hbm, values),
            (query_up_hbm, query_up),
            (key_value_up_hbm, key_value_up),
            (out_down_hbm, out_down),
            (out_up_hbm, out_up),
        )
    ):
        load = pltpu.make_async_copy(source, target, load_sems.at[i])
        load.start()
        loads.append(load)
    (
        keys_load,
        down_load,
        values_load,
        query_up_load,
        key_value_up_load,
        out_down_load,
        out_up_load,
    ) = loads

    barrier = pltpu.get_barrier_semaphore()
    for k in range(1, replicas):
        pl.semaphore_signal(
            barrier,
            inc=1,
            device_id={"replica": ahead(k)},
            device_id_type=pl.DeviceIdType.MESH,
        )
    for t in range(1, tensors):
        pl.semaphore_signal(
            barrier,
            inc=1,
            device_id={"tensor": lax.rem(my_tensor + t, tensors)},
            device_id_type=pl.DeviceIdType.MESH,
        )

    def remote(source, target, sems, i, device):
        copy = pltpu.make_async_remote_copy(
            src_ref=source,
            dst_ref=target,
            send_sem=sems.at[0, i],
            recv_sem=sems.at[1, i],
            device_id=device,
            device_id_type=pl.DeviceIdType.MESH,
        )
        copy.start()
        return copy

    table = table_ref[...]
    table_owner = table // own
    table_local = table - table_owner * own
    pair = jnp.where(iota((8, adapters), 0) == 0, table_owner, table_local)
    adapter_hits = one_hot(iota((adapters, n_rows), 0) == index_ref[...])
    looked_up = mm(pair.astype(F32).astype(BF16), adapter_hits).astype(jnp.int32)
    owner = looked_up[0:1]
    local_slot = looked_up[1:2]
    relative = owner - me
    relative = jnp.where(relative < 0, relative + replicas, relative)
    replica_rows = max(8, replicas)
    owner_hits = iota((replica_rows, n_rows), 0) == relative
    before = one_hot(iota((n_rows, n_rows), 0) <= iota((n_rows, n_rows), 1))
    counts = mm(one_hot(owner_hits), before)
    row_rank = jnp.sum(jnp.where(owner_hits, counts, 0.0), axis=0, keepdims=True) - 1.0
    row_rank = row_rank.astype(jnp.int32)
    row_half = row_rank // half_cap
    row_target = row_half * half_slots + relative * half_cap + row_rank - row_half * half_cap
    placing = one_hot(iota((slots, n_rows), 0) == row_target)
    identity = one_hot(iota((n_rows, n_rows), 0) == iota((n_rows, n_rows), 1))
    unplacing = mm(identity, placing, NT).astype(BF16)
    unplacing_ref[...] = unplacing
    slot_hits = one_hot(iota((LANES, n_rows), 0) == local_slot)
    selectors = mm(placing, slot_hits, NT).astype(BF16)

    packed = mm(placing, feature_ref[...]).astype(BF16)

    def slab(array, half, k):
        at = half * half_slots + k * half_cap
        return array[at : at + half_cap]

    for half in range(halves):
        for k in range(replicas):
            target = feature_send if k else feature_recv
            target[half, k, :, :width] = slab(packed, half, k)
            target[half, k, :, width:] = slab(selectors, half, k)
    pl.semaphore_wait(barrier, replicas + tensors - 2)
    def send_features(half):
        return [
            remote(
                feature_send.at[half, k],
                feature_recv.at[half, k],
                feature_sems.at[half],
                k,
                {"replica": ahead(k)},
            )
            for k in range(1, replicas)
        ]

    feature_copies = [send_features(0)]

    score_rows = n_rows * heads
    block_columns = BLOCK_ROWS * positions
    block_heads = BLOCK_ROWS * heads
    for g in range(groups):
        for h in range(heads):
            column = (g * heads + h) * HEAD_DIM
            base_heads[g, pl.ds(h, n_rows, stride=heads), :] = query_ref[
                :, column : column + HEAD_DIM
            ].astype(F32)
    blocks = n_rows // BLOCK_ROWS
    step_blocks = min(8, blocks)
    steps = blocks // step_blocks
    step_rows = step_blocks * BLOCK_ROWS
    step_heads = step_blocks * block_heads

    def block_of(ref, step, g):
        block = ref[
            pl.ds(pl.multiple_of(step * step_rows, step_rows), step_rows),
            :,
            g * HEAD_DIM : (g + 1) * HEAD_DIM,
        ]
        return block.reshape(step_blocks, block_columns, HEAD_DIM)

    def heads_of(step):
        return pl.ds(pl.multiple_of(step * step_heads, step_heads), step_heads)

    def score(query, key):
        return lax.dot_general(
            query.reshape(step_blocks, block_heads, HEAD_DIM),
            key,
            (((2,), (2,)), ((0,), (0,))),
            preferred_element_type=F32,
        ).reshape(step_heads, block_columns)

    def row_hits(step):
        head_row = iota((step_heads, n_rows), 0) // heads + step * step_rows
        return head_row == iota((step_heads, n_rows), 1)

    lengths = length_ref[...].astype(F32)
    keys_load.wait()

    def base_step(step, carry):
        spread = jnp.where(row_hits(step), lengths, 0.0).astype(BF16)
        head_lengths = mm(spread, jnp.ones((n_rows, block_columns), BF16))
        column = iota((step_heads, block_columns), 1)
        row = iota((step_heads, block_columns), 0)
        valid = ((row // heads) % BLOCK_ROWS == column // positions) & (
            (column % positions).astype(F32) < head_lengths
        )
        for g in range(groups):
            found = score(base_heads[g, heads_of(step), :].astype(BF16), block_of(keys, step, g))
            base_scores[g, heads_of(step), :] = jnp.where(
                valid, found * inverse_root, masked_score
            )
        return carry

    lax.fori_loop(0, steps, base_step, 0)

    for half in range(1, halves):
        for copy in feature_copies[half - 1]:
            copy.wait()
        feature_copies.append(send_features(half))
    key_value_up_load.wait()
    for i in range(2):
        key_value_split[i] = key_value_up[:, i, :]

    down_load.wait()
    query_up_load.wait()
    chooser = one_hot(iota((own, LANES), 0) == iota((own, LANES), 1))

    def fold(terms, selector):
        stacked = terms.reshape(own, terms.shape[0] // own, half_slots)
        return jnp.sum(stacked * selector[:, None, :], axis=0)

    def sum_over_tensor(part, recv, sems):
        recv[0] = part
        copies = [
            remote(
                recv.at[0],
                recv.at[t],
                sems,
                t,
                {"tensor": lax.rem(my_tensor + t, tensors)},
            )
            for t in range(1, tensors)
        ]
        for copy in copies:
            copy.wait()
        total = recv[0]
        for t in range(1, tensors):
            total = total + recv[t]
        return total.astype(BF16).astype(F32)

    def expand(coeffs, selector):
        spread = selector[:, None, :] * coeffs[None, :, :]
        return spread.reshape(own * rank, half_slots).T.astype(BF16)

    half_selectors = []
    delta_copies = []
    for half in range(halves):
        if half == halves - 1:
            for copy in feature_copies[half]:
                copy.wait()
        received = feature_recv[half].reshape(half_slots, -1)
        selector = mm(chooser, received[:, width:], NT)
        half_selectors.append(selector)
        part = fold(mm(down[...], received[:, :width], NT), selector)
        coeffs = sum_over_tensor(part, coeff_recv.at[half], coeff_sems.at[half])
        query_coeffs = expand(coeffs[:rank], selector)
        key_coeffs = expand(coeffs[rank : 2 * rank], selector)
        value_coeffs = expand(coeffs[2 * rank :], selector)
        last = half == halves - 1
        for g in range(groups):
            head_columns = slice(g * HEAD_DIM, (g + 1) * HEAD_DIM)
            sent = [
                mm(query_coeffs, query_up[:, g * group_width : (g + 1) * group_width]),
                mm(key_coeffs, key_value_split[0, :, head_columns]),
                mm(value_coeffs, key_value_split[1, :, head_columns]),
            ]
            sent = jnp.concatenate([x.astype(BF16) for x in sent], axis=1)
            for k in range(replicas):
                target = delta_send if k else delta_recv
                target[half, k, g] = sent[k * half_cap : (k + 1) * half_cap]
            if last:
                delta_copies.append(
                    [
                        remote(
                            delta_send.at[half, k, g],
                            delta_recv.at[half, k, g],
                            delta_sems.at[g],
                            k,
                            {"replica": behind(k)},
                        )
                        for k in reversed(range(1, replicas))
                    ]
                )
        if not last:
            delta_copies.append(
                [
                    remote(
                        delta_send.at[half, k],
                        delta_recv.at[half, k],
                        delta_sems.at[groups + half],
                        k,
                        {"replica": behind(k)},
                    )
                    for k in reversed(range(1, replicas))
                ]
            )

    values_load.wait()
    for copies in delta_copies[: halves - 1]:
        for copy in copies:
            copy.wait()
    context_copies = [[] for _ in range(halves)]

    def send_context(g, parts):
        for part in parts:
            sem = context_sems.at[g if part is None else groups - 1 + part]
            for k in range(1, replicas):
                index = (g, k) if part is None else (g, k, part)
                context_copies[0 if part is None else part].append(
                    remote(
                        context_send.at[index],
                        context_recv.at[index],
                        sem,
                        k,
                        {"replica": ahead(k)},
                    )
                )

    for g in range(groups):
        for copy in delta_copies[halves - 1 + g]:
            copy.wait()
        deltas = 0.0
        for half in range(halves):
            deltas = deltas + mm(
                unplacing[:, half * half_slots : (half + 1) * half_slots],
                delta_recv[half, :, g].reshape(half_slots, -1),
            )
        for h in range(heads):
            delta_heads[pl.ds(h, n_rows, stride=heads), :] = deltas[
                :, h * HEAD_DIM : (h + 1) * HEAD_DIM
            ]
        column = g * HEAD_DIM
        new_key = (
            key_value_ref[:, 0, column : column + HEAD_DIM].astype(F32)
            + adapter_scale * deltas[:, group_width : group_width + HEAD_DIM]
        ).astype(BF16)
        new_value = (
            key_value_ref[:, 1, column : column + HEAD_DIM].astype(F32)
            + adapter_scale * deltas[:, group_width + HEAD_DIM :]
        ).astype(BF16)

        def attend_step(step, carry, g=g, new_key=new_key, new_value=new_value):
            here = heads_of(step)
            plain = base_heads[g, here, :].astype(BF16)
            correction = delta_heads[here, :].astype(BF16)
            scores = base_scores[g, here, :] + (adapter_scale * inverse_root) * score(
                correction, block_of(keys, step, g)
            )
            own_scores = (
                mm(plain, new_key, NT) + adapter_scale * mm(correction, new_key, NT)
            ) * inverse_root
            own_scores = jnp.where(row_hits(step), own_scores, masked_score)
            peak = jnp.maximum(
                jnp.max(scores, axis=1, keepdims=True), jnp.max(own_scores, axis=1, keepdims=True)
            )
            cache_exp = jnp.exp(scores - peak)
            own_exp = jnp.exp(own_scores - peak)
            total = jnp.sum(cache_exp, axis=1, keepdims=True) + jnp.sum(
                own_exp, axis=1, keepdims=True
            )
            share = 1.0 / total
            weights = (cache_exp * share).astype(BF16)
            own_weights = (own_exp * share).astype(BF16)
            found = lax.dot_general(
                weights.reshape(step_blocks, block_heads, block_columns),
                block_of(values, step, g),
                (((2,), (1,)), ((0,), (0,))),
                preferred_element_type=F32,
            ).reshape(step_heads, HEAD_DIM)
            context_heads[here, :] = found + mm(own_weights, new_value)
            return carry

        lax.fori_loop(0, steps, attend_step, 0)
        for h in range(heads):
            column = (g * heads + h) * HEAD_DIM
            context_ref[:, column : column + HEAD_DIM] = context_heads[
                pl.ds(h, n_rows, stride=heads), :
            ].astype(BF16)
        packed = mm(placing, context_ref[:, g * group_width : (g + 1) * group_width]).astype(BF16)
        for half in range(halves):
            for k in range(replicas):
                target = context_send if k else context_recv
                target[g, k, half] = slab(packed, half, k)
        if g < groups - 1:
            send_context(g, [None])
    send_context(groups - 1, [0])

    out_down_load.wait()
    out_up_load.wait()
    adjust_copies = []
    for half in range(halves):
        for copy in context_copies[half]:
            copy.wait()
        if half < halves - 1:
            send_context(groups - 1, [half + 1])
        terms = 0.0
        for g in range(groups):
            terms = terms + mm(
                out_down[:, g * group_width : (g + 1) * group_width],
                context_recv[g, :, half].reshape(half_slots, group_width),
                NT,
            )
        selector = half_selectors[half]
        coeffs = sum_over_tensor(
            fold(terms, selector), out_coeff_recv.at[half], out_coeff_sems.at[half]
        )
        sent = (adapter_scale * mm(expand(coeffs, selector), out_up[...])).astype(BF16)
        for k in range(replicas):
            adjust_send[half, k] = sent[k * half_cap : (k + 1) * half_cap]
        kept = pltpu.make_async_copy(
            adjust_send.at[half, 0], adjust_recv.at[half, 0], keep_sems.at[half]
        )
        kept.start()
        adjust_copies.append(kept)
        adjust_copies += [
            remote(
                adjust_send.at[half, k],
                adjust_recv.at[half, k],
                adjust_sems.at[half],
                k,
                {"replica": behind(k)},
            )
            for k in reversed(range(1, replicas))
        ]
    for copy in adjust_copies:
        copy.wait()


def finish(context_ref, received_ref, unplacing_ref, context_out, adjust_ref):
    context_out[...] = context_ref[...]
    adjust_ref[...] = mm(
        unplacing_ref[...], received_ref[...].reshape(-1, adjust_ref.shape[1])
    ).astype(BF16)


def local(
    replicas,
    tensors,
    features,
    base_query,
    base_key_value,
    cached_key_rows,
    cached_value_rows,
    cache_length,
    row_adapter_index,
    adapter_storage_slot,
    adapter_down_maps,
    query_up_maps,
    key_value_up_maps,
    output_down_maps,
    output_up_maps,
):
    n_rows, width = features.shape
    own, coeff_width, _ = adapter_down_maps.shape
    rank = coeff_width // 3
    query_width = base_query.shape[1]
    kv_width = base_key_value.shape[2]
    positions = cached_key_rows.shape[1]
    groups = kv_width // HEAD_DIM
    heads = query_width // HEAD_DIM // groups
    group_width = heads * HEAD_DIM
    delta_width = group_width + 2 * HEAD_DIM
    capacity = min(n_rows // 2, 2 * n_rows // replicas)
    cap = -(-capacity // 16) * 16
    halves = 2 if cap % 32 == 0 else 1
    half_cap = cap // halves
    half_slots = replicas * half_cap
    slots = replicas * cap
    score_rows = n_rows * heads

    vmem = pl.BlockSpec(memory_space=pltpu.VMEM)
    anywhere = pl.BlockSpec(memory_space=pl.ANY)

    def pair_sems(*lead):
        return pltpu.SemaphoreType.DMA((*lead, 2, replicas))

    context, received, unplacing = pl.pallas_call(
        functools.partial(kernel, replicas, tensors, cap, halves, rank),
        out_shape=(
            jax.ShapeDtypeStruct((n_rows, query_width), BF16),
            jax.ShapeDtypeStruct((halves, replicas, half_cap, query_width), BF16),
            jax.ShapeDtypeStruct((n_rows, slots), BF16),
        ),
        in_specs=[vmem] * 6 + [anywhere] * 7,
        out_specs=(vmem, anywhere, vmem),
        scratch_shapes=[
            pltpu.VMEM(cached_key_rows.shape, BF16),
            pltpu.VMEM(cached_value_rows.shape, BF16),
            pltpu.VMEM((own * coeff_width, width), BF16),
            pltpu.VMEM((own * rank, query_width), BF16),
            pltpu.VMEM((own * rank, 2, kv_width), BF16),
            pltpu.VMEM((2, own * rank, kv_width), BF16),
            pltpu.VMEM((own * rank, query_width), BF16),
            pltpu.VMEM((own * rank, query_width), BF16),
            pltpu.VMEM((halves, replicas, half_cap, width + LANES), BF16),
            pltpu.VMEM((halves, replicas, half_cap, width + LANES), BF16),
            pltpu.VMEM((halves, tensors, coeff_width, half_slots), F32),
            pltpu.VMEM((halves, replicas, groups, half_cap, delta_width), BF16),
            pltpu.VMEM((halves, replicas, groups, half_cap, delta_width), BF16),
            pltpu.VMEM((groups, replicas, halves, half_cap, group_width), BF16),
            pltpu.VMEM((groups, replicas, halves, half_cap, group_width), BF16),
            pltpu.VMEM((halves, tensors, rank, half_slots), F32),
            pltpu.VMEM((halves, replicas, half_cap, query_width), BF16),
            pltpu.VMEM((groups, score_rows, HEAD_DIM), F32),
            pltpu.VMEM((score_rows, HEAD_DIM), F32),
            pltpu.VMEM((score_rows, HEAD_DIM), F32),
            pltpu.VMEM((groups, score_rows, BLOCK_ROWS * positions), F32),
            pltpu.SemaphoreType.DMA((7,)),
            pair_sems(halves),
            pltpu.SemaphoreType.DMA((halves, 2, tensors)),
            pair_sems(groups + halves - 1),
            pair_sems(groups + halves - 1),
            pltpu.SemaphoreType.DMA((halves, 2, tensors)),
            pair_sems(halves),
            pltpu.SemaphoreType.DMA((halves,)),
        ],
        compiler_params=pltpu.CompilerParams(
            collective_id=0, has_side_effects=True, vmem_limit_bytes=56 * 1024 * 1024
        ),
    )(
        row_adapter_index.reshape(1, -1),
        adapter_storage_slot.reshape(1, -1),
        cache_length.reshape(1, -1),
        features,
        base_query,
        base_key_value,
        cached_key_rows,
        cached_value_rows,
        adapter_down_maps.reshape(own * coeff_width, width),
        query_up_maps.reshape(own * rank, query_width),
        key_value_up_maps.reshape(own * rank, 2, kv_width),
        output_down_maps.reshape(own * rank, query_width),
        output_up_maps.reshape(own * rank, query_width),
    )
    return pl.pallas_call(
        finish,
        out_shape=(
            jax.ShapeDtypeStruct((n_rows, query_width), BF16),
            jax.ShapeDtypeStruct((n_rows, query_width), BF16),
        ),
        in_specs=[vmem] * 3,
        out_specs=(vmem, vmem),
        compiler_params=pltpu.CompilerParams(vmem_limit_bytes=56 * 1024 * 1024),
    )(context, received, unplacing)


def solution(mesh):
    return jax.shard_map(
        functools.partial(local, mesh.shape["replica"], mesh.shape["tensor"]),
        mesh=mesh,
        in_specs=(
            P(("groups", "replica"), "tensor"),
            P(("groups", "replica"), "tensor"),
            P(("groups", "replica"), None, "tensor"),
            P(("groups", "replica"), None, "tensor"),
            P(("groups", "replica"), None, "tensor"),
            P(("groups", "replica")),
            P(("groups", "replica")),
            P("groups"),
            P("replica", None, "tensor"),
            P("replica", None, "tensor"),
            P("replica", None, None, "tensor"),
            P("replica", None, "tensor"),
            P("replica", None, "tensor"),
        ),
        out_specs=(P(("groups", "replica"), "tensor"), P(("groups", "replica"), "tensor")),
        check_vma=False,
    )
```

```python
import functools
import math

import jax
import jax.numpy as jnp
from jax import lax
from jax.experimental import pallas as pl
from jax.experimental.pallas import tpu as pltpu
from jax.sharding import PartitionSpec as P

HEAD_DIM = 128
LANES = 128
BLOCK_ROWS = 4

adapter_scale = 2.0
masked_score = -1e30
BF16 = jnp.bfloat16
F32 = jnp.float32

NN = (((1,), (0,)), ((), ()))
NT = (((1,), (1,)), ((), ()))


def mm(a, b, dims=NN):
    return lax.dot_general(a, b, dims, preferred_element_type=F32)


def iota(shape, dim):
    return lax.broadcasted_iota(jnp.int32, shape, dim)


def one_hot(hit):
    return jnp.where(hit, 1.0, 0.0).astype(BF16)


def kernel(
    replicas,
    tensors,
    cap,
    halves,
    rank,
    index_ref,
    table_ref,
    length_ref,
    feature_ref,
    query_ref,
    key_value_ref,
    key_hbm,
    value_hbm,
    down_hbm,
    query_up_hbm,
    key_value_up_hbm,
    out_down_hbm,
    out_up_hbm,
    context_ref,
    adjust_recv,
    unplacing_ref,
    keys,
    values,
    down,
    query_up,
    key_value_up,
    key_value_split,
    out_down,
    out_up,
    feature_send,
    feature_recv,
    coeff_recv,
    delta_send,
    delta_recv,
    context_send,
    context_recv,
    out_coeff_recv,
    adjust_send,
    base_heads,
    delta_heads,
    context_heads,
    base_scores,
    load_sems,
    feature_sems,
    coeff_sems,
    delta_sems,
    context_sems,
    out_coeff_sems,
    adjust_sems,
    keep_sems,
):
    n_rows, width = feature_ref.shape
    query_width = query_ref.shape[1]
    kv_width = key_value_ref.shape[2]
    groups = kv_width // HEAD_DIM
    heads = query_width // HEAD_DIM // groups
    group_width = heads * HEAD_DIM
    positions = key_hbm.shape[1]
    adapters = table_ref.shape[1]
    own = out_down_hbm.shape[0] // rank
    half_cap = cap // halves
    half_slots = replicas * half_cap
    slots = replicas * cap
    inverse_root = 1.0 / math.sqrt(HEAD_DIM)
    me = lax.axis_index("replica")
    my_tensor = lax.axis_index("tensor")

    def ahead(k):
        return lax.rem(me + k, replicas)

    def behind(k):
        return lax.rem(me + replicas - k, replicas)

    loads = []
    for i, (source, target) in enumerate(
        (
            (key_hbm, keys),
            (down_hbm, down),
            (value_hbm, values),
            (query_up_hbm, query_up),
            (key_value_up_hbm, key_value_up),
            (out_down_hbm, out_down),
            (out_up_hbm, out_up),
        )
    ):
        load = pltpu.make_async_copy(source, target, load_sems.at[i])
        load.start()
        loads.append(load)
    (
        keys_load,
        down_load,
        values_load,
        query_up_load,
        key_value_up_load,
        out_down_load,
        out_up_load,
    ) = loads

    barrier = pltpu.get_barrier_semaphore()
    for k in range(1, replicas):
        pl.semaphore_signal(
            barrier,
            inc=1,
            device_id={"replica": ahead(k)},
            device_id_type=pl.DeviceIdType.MESH,
        )
    for t in range(1, tensors):
        pl.semaphore_signal(
            barrier,
            inc=1,
            device_id={"tensor": lax.rem(my_tensor + t, tensors)},
            device_id_type=pl.DeviceIdType.MESH,
        )

    def remote(source, target, sems, i, device):
        copy = pltpu.make_async_remote_copy(
            src_ref=source,
            dst_ref=target,
            send_sem=sems.at[0, i],
            recv_sem=sems.at[1, i],
            device_id=device,
            device_id_type=pl.DeviceIdType.MESH,
        )
        copy.start()
        return copy

    table = table_ref[...]
    table_owner = table // own
    table_local = table - table_owner * own
    pair = jnp.where(iota((8, adapters), 0) == 0, table_owner, table_local)
    adapter_hits = one_hot(iota((adapters, n_rows), 0) == index_ref[...])
    looked_up = mm(pair.astype(F32).astype(BF16), adapter_hits).astype(jnp.int32)
    owner = looked_up[0:1]
    local_slot = looked_up[1:2]
    relative = owner - me
    relative = jnp.where(relative < 0, relative + replicas, relative)
    replica_rows = max(8, replicas)
    owner_hits = iota((replica_rows, n_rows), 0) == relative
    before = one_hot(iota((n_rows, n_rows), 0) <= iota((n_rows, n_rows), 1))
    counts = mm(one_hot(owner_hits), before)
    row_rank = jnp.sum(jnp.where(owner_hits, counts, 0.0), axis=0, keepdims=True) - 1.0
    row_rank = row_rank.astype(jnp.int32)
    row_half = row_rank // half_cap
    row_target = row_half * half_slots + relative * half_cap + row_rank - row_half * half_cap
    placing = one_hot(iota((slots, n_rows), 0) == row_target)
    slot_hits = [
        one_hot(iota((LANES, n_rows), 0) == local_slot + half * own) for half in range(halves)
    ]


    def slab(array, half, k):
        at = half * half_slots + k * half_cap
        return array[at : at + half_cap]

    def pack_features(half):
        chosen = placing[half * half_slots : (half + 1) * half_slots]
        packed = mm(chosen, feature_ref[...]).astype(BF16)
        for k in range(replicas):
            target = feature_send if k else feature_recv
            target[half, k, :, :width] = packed[k * half_cap : (k + 1) * half_cap]

    selectors = 0.0
    for half in range(halves):
        chosen = placing[half * half_slots : (half + 1) * half_slots]
        selectors = selectors + mm(chosen, slot_hits[half], NT)
    selectors = selectors.astype(BF16)
    for k in range(replicas):
        target = feature_send if k else feature_recv
        target[0, k, :, width:] = selectors[k * half_cap : (k + 1) * half_cap]
    pack_features(0)
    pl.semaphore_wait(barrier, replicas + tensors - 2)
    def send_features(half):
        return [
            remote(
                feature_send.at[half, k, :, pl.ds(0, width if half else width + LANES)],
                feature_recv.at[half, k, :, pl.ds(0, width if half else width + LANES)],
                feature_sems.at[half],
                k,
                {"replica": ahead(k)},
            )
            for k in range(1, replicas)
        ]

    feature_copies = [send_features(0)]
    for half in range(1, halves):
        pack_features(half)
    identity = one_hot(iota((n_rows, n_rows), 0) == iota((n_rows, n_rows), 1))
    unplacing = mm(identity, placing, NT).astype(BF16)
    unplacing_ref[...] = unplacing

    score_rows = n_rows * heads
    block_columns = BLOCK_ROWS * positions
    block_heads = BLOCK_ROWS * heads
    for g in range(groups):
        for h in range(heads):
            column = (g * heads + h) * HEAD_DIM
            base_heads[g, pl.ds(h, n_rows, stride=heads), :] = query_ref[
                :, column : column + HEAD_DIM
            ].astype(F32)
    blocks = n_rows // BLOCK_ROWS
    step_blocks = min(8, blocks)
    steps = blocks // step_blocks
    step_rows = step_blocks * BLOCK_ROWS
    step_heads = step_blocks * block_heads

    def block_of(ref, step, g):
        block = ref[
            pl.ds(pl.multiple_of(step * step_rows, step_rows), step_rows),
            :,
            g * HEAD_DIM : (g + 1) * HEAD_DIM,
        ]
        return block.reshape(step_blocks, block_columns, HEAD_DIM)

    def heads_of(step):
        return pl.ds(pl.multiple_of(step * step_heads, step_heads), step_heads)

    def score(query, key):
        return lax.dot_general(
            query.reshape(step_blocks, block_heads, HEAD_DIM),
            key,
            (((2,), (2,)), ((0,), (0,))),
            preferred_element_type=F32,
        ).reshape(step_heads, block_columns)

    def row_hits(step):
        head_row = iota((step_heads, n_rows), 0) // heads + step * step_rows
        return head_row == iota((step_heads, n_rows), 1)

    lengths = length_ref[...].astype(F32)
    keys_load.wait()

    def base_step(step, carry):
        spread = jnp.where(row_hits(step), lengths, 0.0).astype(BF16)
        head_lengths = mm(spread, jnp.ones((n_rows, block_columns), BF16))
        column = iota((step_heads, block_columns), 1)
        row = iota((step_heads, block_columns), 0)
        valid = ((row // heads) % BLOCK_ROWS == column // positions) & (
            (column % positions).astype(F32) < head_lengths
        )
        for g in range(groups):
            found = score(base_heads[g, heads_of(step), :].astype(BF16), block_of(keys, step, g))
            base_scores[g, heads_of(step), :] = jnp.where(
                valid, found * inverse_root, masked_score
            )
        return carry

    lax.fori_loop(0, steps, base_step, 0)

    key_value_up_load.wait()
    for i in range(2):
        key_value_split[i] = key_value_up[:, i, :]

    for half in range(1, halves):
        for copy in feature_copies[half - 1]:
            copy.wait()
        feature_copies.append(send_features(half))
    down_load.wait()
    query_up_load.wait()

    def fold(terms, selector):
        stacked = terms.reshape(own, terms.shape[0] // own, half_slots)
        return jnp.sum(stacked * selector[:, None, :], axis=0)

    def sum_over_tensor(part, recv, sems):
        recv[0] = part
        copies = [
            remote(
                recv.at[0],
                recv.at[t],
                sems,
                t,
                {"tensor": lax.rem(my_tensor + t, tensors)},
            )
            for t in range(1, tensors)
        ]
        for copy in copies:
            copy.wait()
        total = recv[0]
        for t in range(1, tensors):
            total = total + recv[t]
        return total.astype(BF16).astype(F32)

    def expand(coeffs, selector):
        spread = selector[:, None, :] * coeffs[None, :, :]
        return spread.reshape(own * rank, half_slots).T.astype(BF16)

    half_selectors = []
    delta_copies = []
    for half in range(halves):
        if half == halves - 1:
            for copy in feature_copies[half]:
                copy.wait()
        received = feature_recv[half].reshape(half_slots, -1)
        chooser = one_hot(iota((own, LANES), 0) + half * own == iota((own, LANES), 1))
        selector = mm(chooser, feature_recv[0].reshape(half_slots, -1)[:, width:], NT)
        half_selectors.append(selector)
        part = fold(mm(down[...], received[:, :width], NT), selector)
        coeffs = sum_over_tensor(part, coeff_recv.at[half], coeff_sems.at[half])
        query_coeffs = expand(coeffs[:rank], selector)
        key_coeffs = expand(coeffs[rank : 2 * rank], selector)
        value_coeffs = expand(coeffs[2 * rank :], selector)
        last = half == halves - 1
        for g in range(groups):
            head_columns = slice(g * HEAD_DIM, (g + 1) * HEAD_DIM)
            sent = [
                mm(query_coeffs, query_up[:, g * group_width : (g + 1) * group_width]),
                mm(key_coeffs, key_value_split[0, :, head_columns]),
                mm(value_coeffs, key_value_split[1, :, head_columns]),
            ]
            sent = jnp.concatenate([x.astype(BF16) for x in sent], axis=1)
            for k in range(replicas):
                target = delta_send if k else delta_recv
                target[half, k, g] = sent[k * half_cap : (k + 1) * half_cap]
            if last:
                delta_copies.append(
                    [
                        remote(
                            delta_send.at[half, k, g],
                            delta_recv.at[half, k, g],
                            delta_sems.at[g],
                            k,
                            {"replica": behind(k)},
                        )
                        for k in reversed(range(1, replicas))
                    ]
                )
        if not last:
            delta_copies.append(
                [
                    remote(
                        delta_send.at[half, k],
                        delta_recv.at[half, k],
                        delta_sems.at[groups + half],
                        k,
                        {"replica": behind(k)},
                    )
                    for k in reversed(range(1, replicas))
                ]
            )

    values_load.wait()
    for copies in delta_copies[: halves - 1]:
        for copy in copies:
            copy.wait()
    context_copies = [[] for _ in range(halves)]

    def send_context(g, parts):
        for part in parts:
            sem = context_sems.at[g if part is None else groups - 1 + part]
            for k in range(1, replicas):
                index = (g, k) if part is None else (g, k, part)
                context_copies[0 if part is None else part].append(
                    remote(
                        context_send.at[index],
                        context_recv.at[index],
                        sem,
                        k,
                        {"replica": ahead(k)},
                    )
                )

    for g in range(groups):
        for copy in delta_copies[halves - 1 + g]:
            copy.wait()
        deltas = 0.0
        for half in range(halves):
            deltas = deltas + mm(
                unplacing[:, half * half_slots : (half + 1) * half_slots],
                delta_recv[half, :, g].reshape(half_slots, -1),
            )
        for h in range(heads):
            delta_heads[pl.ds(h, n_rows, stride=heads), :] = deltas[
                :, h * HEAD_DIM : (h + 1) * HEAD_DIM
            ]
        column = g * HEAD_DIM
        new_key = (
            key_value_ref[:, 0, column : column + HEAD_DIM].astype(F32)
            + adapter_scale * deltas[:, group_width : group_width + HEAD_DIM]
        ).astype(BF16)
        new_value = (
            key_value_ref[:, 1, column : column + HEAD_DIM].astype(F32)
            + adapter_scale * deltas[:, group_width + HEAD_DIM :]
        ).astype(BF16)

        def attend_step(step, carry, g=g, new_key=new_key, new_value=new_value):
            here = heads_of(step)
            plain = base_heads[g, here, :].astype(BF16)
            correction = delta_heads[here, :].astype(BF16)
            scores = base_scores[g, here, :] + (adapter_scale * inverse_root) * score(
                correction, block_of(keys, step, g)
            )
            own_scores = (
                mm(plain, new_key, NT) + adapter_scale * mm(correction, new_key, NT)
            ) * inverse_root
            own_scores = jnp.where(row_hits(step), own_scores, masked_score)
            peak = jnp.maximum(
                jnp.max(scores, axis=1, keepdims=True), jnp.max(own_scores, axis=1, keepdims=True)
            )
            cache_exp = jnp.exp(scores - peak)
            own_exp = jnp.exp(own_scores - peak)
            total = jnp.sum(cache_exp, axis=1, keepdims=True) + jnp.sum(
                own_exp, axis=1, keepdims=True
            )
            share = 1.0 / total
            weights = (cache_exp * share).astype(BF16)
            own_weights = (own_exp * share).astype(BF16)
            found = lax.dot_general(
                weights.reshape(step_blocks, block_heads, block_columns),
                block_of(values, step, g),
                (((2,), (1,)), ((0,), (0,))),
                preferred_element_type=F32,
            ).reshape(step_heads, HEAD_DIM)
            context_heads[here, :] = found + mm(own_weights, new_value)
            return carry

        lax.fori_loop(0, steps, attend_step, 0)
        for h in range(heads):
            column = (g * heads + h) * HEAD_DIM
            context_ref[:, column : column + HEAD_DIM] = context_heads[
                pl.ds(h, n_rows, stride=heads), :
            ].astype(BF16)
        packed = mm(placing, context_ref[:, g * group_width : (g + 1) * group_width]).astype(BF16)
        for half in range(halves):
            for k in range(replicas):
                target = context_send if k else context_recv
                target[g, k, half] = slab(packed, half, k)
        if g < groups - 1:
            send_context(g, [None])
    send_context(groups - 1, [0])

    out_down_load.wait()
    out_up_load.wait()
    adjust_copies = []
    for half in range(halves):
        for copy in context_copies[half]:
            copy.wait()
        if half < halves - 1:
            send_context(groups - 1, [half + 1])
        terms = 0.0
        for g in range(groups):
            terms = terms + mm(
                out_down[:, g * group_width : (g + 1) * group_width],
                context_recv[g, :, half].reshape(half_slots, group_width),
                NT,
            )
        selector = half_selectors[half]
        coeffs = sum_over_tensor(
            fold(terms, selector), out_coeff_recv.at[half], out_coeff_sems.at[half]
        )
        sent = (adapter_scale * mm(expand(coeffs, selector), out_up[...])).astype(BF16)
        for k in range(replicas):
            adjust_send[half, k] = sent[k * half_cap : (k + 1) * half_cap]
        kept = pltpu.make_async_copy(
            adjust_send.at[half, 0], adjust_recv.at[half, 0], keep_sems.at[half]
        )
        kept.start()
        adjust_copies.append(kept)
        adjust_copies += [
            remote(
                adjust_send.at[half, k],
                adjust_recv.at[half, k],
                adjust_sems.at[half],
                k,
                {"replica": behind(k)},
            )
            for k in reversed(range(1, replicas))
        ]
    for copy in adjust_copies:
        copy.wait()


def finish(context_ref, received_ref, unplacing_ref, context_out, adjust_ref):
    context_out[...] = context_ref[...]
    adjust_ref[...] = mm(
        unplacing_ref[...], received_ref[...].reshape(-1, adjust_ref.shape[1])
    ).astype(BF16)


def local(
    replicas,
    tensors,
    features,
    base_query,
    base_key_value,
    cached_key_rows,
    cached_value_rows,
    cache_length,
    row_adapter_index,
    adapter_storage_slot,
    adapter_down_maps,
    query_up_maps,
    key_value_up_maps,
    output_down_maps,
    output_up_maps,
):
    n_rows, width = features.shape
    own, coeff_width, _ = adapter_down_maps.shape
    rank = coeff_width // 3
    query_width = base_query.shape[1]
    kv_width = base_key_value.shape[2]
    positions = cached_key_rows.shape[1]
    groups = kv_width // HEAD_DIM
    heads = query_width // HEAD_DIM // groups
    group_width = heads * HEAD_DIM
    delta_width = group_width + 2 * HEAD_DIM
    capacity = min(n_rows // 2, 2 * n_rows // replicas)
    cap = -(-capacity // 16) * 16
    halves = 2 if cap % 32 == 0 else 1
    half_cap = cap // halves
    half_slots = replicas * half_cap
    slots = replicas * cap
    score_rows = n_rows * heads

    vmem = pl.BlockSpec(memory_space=pltpu.VMEM)
    anywhere = pl.BlockSpec(memory_space=pl.ANY)

    def pair_sems(*lead):
        return pltpu.SemaphoreType.DMA((*lead, 2, replicas))

    context, received, unplacing = pl.pallas_call(
        functools.partial(kernel, replicas, tensors, cap, halves, rank),
        out_shape=(
            jax.ShapeDtypeStruct((n_rows, query_width), BF16),
            jax.ShapeDtypeStruct((halves, replicas, half_cap, query_width), BF16),
            jax.ShapeDtypeStruct((n_rows, slots), BF16),
        ),
        in_specs=[vmem] * 6 + [anywhere] * 7,
        out_specs=(vmem, anywhere, vmem),
        scratch_shapes=[
            pltpu.VMEM(cached_key_rows.shape, BF16),
            pltpu.VMEM(cached_value_rows.shape, BF16),
            pltpu.VMEM((own * coeff_width, width), BF16),
            pltpu.VMEM((own * rank, query_width), BF16),
            pltpu.VMEM((own * rank, 2, kv_width), BF16),
            pltpu.VMEM((2, own * rank, kv_width), BF16),
            pltpu.VMEM((own * rank, query_width), BF16),
            pltpu.VMEM((own * rank, query_width), BF16),
            pltpu.VMEM((halves, replicas, half_cap, width + LANES), BF16),
            pltpu.VMEM((halves, replicas, half_cap, width + LANES), BF16),
            pltpu.VMEM((halves, tensors, coeff_width, half_slots), F32),
            pltpu.VMEM((halves, replicas, groups, half_cap, delta_width), BF16),
            pltpu.VMEM((halves, replicas, groups, half_cap, delta_width), BF16),
            pltpu.VMEM((groups, replicas, halves, half_cap, group_width), BF16),
            pltpu.VMEM((groups, replicas, halves, half_cap, group_width), BF16),
            pltpu.VMEM((halves, tensors, rank, half_slots), F32),
            pltpu.VMEM((halves, replicas, half_cap, query_width), BF16),
            pltpu.VMEM((groups, score_rows, HEAD_DIM), F32),
            pltpu.VMEM((score_rows, HEAD_DIM), F32),
            pltpu.VMEM((score_rows, HEAD_DIM), F32),
            pltpu.VMEM((groups, score_rows, BLOCK_ROWS * positions), F32),
            pltpu.SemaphoreType.DMA((7,)),
            pair_sems(halves),
            pltpu.SemaphoreType.DMA((halves, 2, tensors)),
            pair_sems(groups + halves - 1),
            pair_sems(groups + halves - 1),
            pltpu.SemaphoreType.DMA((halves, 2, tensors)),
            pair_sems(halves),
            pltpu.SemaphoreType.DMA((halves,)),
        ],
        compiler_params=pltpu.CompilerParams(
            collective_id=0, has_side_effects=True, vmem_limit_bytes=56 * 1024 * 1024
        ),
    )(
        row_adapter_index.reshape(1, -1),
        adapter_storage_slot.reshape(1, -1),
        cache_length.reshape(1, -1),
        features,
        base_query,
        base_key_value,
        cached_key_rows,
        cached_value_rows,
        adapter_down_maps.reshape(own * coeff_width, width),
        query_up_maps.reshape(own * rank, query_width),
        key_value_up_maps.reshape(own * rank, 2, kv_width),
        output_down_maps.reshape(own * rank, query_width),
        output_up_maps.reshape(own * rank, query_width),
    )
    return pl.pallas_call(
        finish,
        out_shape=(
            jax.ShapeDtypeStruct((n_rows, query_width), BF16),
            jax.ShapeDtypeStruct((n_rows, query_width), BF16),
        ),
        in_specs=[vmem] * 3,
        out_specs=(vmem, vmem),
        compiler_params=pltpu.CompilerParams(vmem_limit_bytes=56 * 1024 * 1024),
    )(context, received, unplacing)


def solution(mesh):
    return jax.shard_map(
        functools.partial(local, mesh.shape["replica"], mesh.shape["tensor"]),
        mesh=mesh,
        in_specs=(
            P(("groups", "replica"), "tensor"),
            P(("groups", "replica"), "tensor"),
            P(("groups", "replica"), None, "tensor"),
            P(("groups", "replica"), None, "tensor"),
            P(("groups", "replica"), None, "tensor"),
            P(("groups", "replica")),
            P(("groups", "replica")),
            P("groups"),
            P("replica", None, "tensor"),
            P("replica", None, "tensor"),
            P("replica", None, None, "tensor"),
            P("replica", None, "tensor"),
            P("replica", None, "tensor"),
        ),
        out_specs=(P(("groups", "replica"), "tensor"), P(("groups", "replica"), "tensor")),
        check_vma=False,
    )
```
